32 devices in a mesh: seq: 8 (over z, x), chan: 4 (over y, core).
Axes of the slice: x: 2, y: 2, z: 4, core: 2. Of those that a mesh axis runs over, the one named last changes fastest.
Arguments:
- projected: bfloat16 [3, 2048, 2048], P(None, 'seq', 'chan'), may hold values from -6 to 6
- short_taps: float32 [3, 3, 2048], P(None, None, 'chan'), may hold values from -3 to 3
- skip_gain: float32 [2048], P('chan'), may hold values from 0.5 to 1.5
- filter_response: float32 [2, 4096, 2048], P(None, 'seq', 'chan'), may hold values from -6 to 6
- out_weight: bfloat16 [2048, 8192], P('chan'), may hold values from -0.1875 to 0.1875
Outputs:
- mixed: bfloat16 [2048, 8192], P('seq', 'chan')
The draws below stay inside these ranges and needn't reach their ends.
All inputs are finite; a program needn't handle non-finite values.
Results may differ from the reference program's by a relative error of at most 0.015.
Values may be sent and summed in bfloat16 or wider, within the bound.
A program may use at most 64 MiB of HBM per device.

```python
import math
import jax
import jax.numpy as jnp
from jax import lax

D = 8192
C = 2048
SEQ_LEN = 2048
FFT_LEN = 4096


def strengthened(result, key, source, target, parts, factor):
    def block_of(dim):
        return (jnp.arange(result.shape[dim]) // (result.shape[dim] // parts)).reshape((-1,) + (1,) * (result.ndim - 1 - dim))

    one_side = jax.random.permutation(key, parts)[block_of(target)]
    far = (block_of(target) + parts // 2) % parts
    return jnp.where((block_of(source) == one_side) | (block_of(source) == far), factor * result, result)


def block_scale(stream_key, dims, shards, low, top_value):
    factor_of = 1.0
    for axis_at, shards_of in shards:
        steps = jax.random.uniform(jax.random.fold_in(jax.random.fold_in(stream_key, 6), axis_at), (shards_of,), jnp.float32, low / len(shards), top_value / len(shards))
        factor_of = factor_of * jnp.repeat(jnp.exp(steps), dims[axis_at] // shards_of).reshape((-1,) + (1,) * (len(dims) - 1 - axis_at))
    return factor_of


def scatter_about(rng, extent, width, reach, shards=(), dtype=jnp.bfloat16):
    result = jax.random.normal(rng, extent, jnp.float32) * width
    if len(shards) > 0:
        result = block_scale(rng, extent, shards, -0.22, 0.18) * result
    return jnp.clip(result, min=-reach, max=reach).astype(dtype)


def gaussian_with(own_key, shape, scale, limit, cuts, heavy, held_as=jnp.bfloat16):
    array = scale * jax.random.normal(own_key, shape, jnp.float32)
    if cuts:
        array = array * block_scale(own_key, shape, cuts, -0.22, 0.18)
    return jnp.clip(strengthened(array, jax.random.fold_in(own_key, 3), *heavy), -limit, limit).astype(held_as)


def setup_inputs(seed: int = 0) -> dict:
    seeds = jax.random.split(jax.random.key(seed), 6)
    projected = scatter_about(seeds[0], (3, SEQ_LEN, C), 1.0, 6.0, ((1, 8), (2, 4)))
    short_taps = scatter_about(seeds[1], (3, 3, C), 0.6, 3.0, ((2, 4),), jnp.float32)
    skip_gain = jnp.clip(0.5 + 1.0 * jax.random.uniform(seeds[2], (C,), jnp.float32) ** block_scale(seeds[2], (C,), ((0, 4),), -0.2, 0.2), 0.5, 1.5)
    filter_response = scatter_about(seeds[3], (2, FFT_LEN, C), 1.0, 6.0, ((1, 8), (2, 4)), jnp.float32)
    out_weight = gaussian_with(seeds[4], (C, D), C ** -0.5, 0.1875, ((0, 4),), (0, 1, 4, 2.0))
    return dict(projected=projected, short_taps=short_taps, skip_gain=skip_gain, filter_response=filter_response, out_weight=out_weight)


def long_filter(signal, response):
    group_width = math.gcd(C, 256)
    groups = C // group_width
    signal_blocks = jnp.transpose(signal.reshape(SEQ_LEN, groups, group_width), (1, 0, 2))
    response_blocks = jnp.transpose(response.reshape(2, FFT_LEN, groups, group_width), (2, 0, 1, 3))

    def one_group(pair):
        sig_part, resp_part = pair
        spectrum = jnp.fft.fft(sig_part, n=FFT_LEN, axis=0)
        kernel = lax.complex(resp_part[0], resp_part[1])
        return jnp.real(jnp.fft.ifft(spectrum * kernel, axis=0)[:SEQ_LEN])

    filtered = lax.map(one_group, (signal_blocks, response_blocks))
    return jnp.transpose(filtered, (1, 0, 2)).reshape(SEQ_LEN, C)


def reference(projected, short_taps, skip_gain, filter_response, out_weight):
    values = projected.astype(jnp.float32)
    padded = jnp.pad(values, ((0, 0), (2, 0), (0, 0)))
    shaped = (short_taps[:, 0, None, :] * padded[:, 2:]
              + short_taps[:, 1, None, :] * padded[:, 1:-1]
              + short_taps[:, 2, None, :] * padded[:, :-2])
    query = shaped[0]
    signal = shaped[1] * shaped[2]
    filtered = long_filter(signal, filter_response)
    gated = (query * (filtered + skip_gain[None, :] * signal)).astype(jnp.bfloat16)
    return jnp.dot(gated, out_weight, preferred_element_type=jnp.float32).astype(jnp.bfloat16)
```

```python
import functools
import math

import jax
import jax.numpy as jnp
import numpy as np
from jax import lax
from jax.experimental import pallas as pl
from jax.experimental.pallas import tpu as pltpu
from jax.sharding import PartitionSpec as P

LANES = 128
MESH = pl.DeviceIdType.MESH


def dft_tables(rows, parts):
    coarse = 2 * parts
    total = coarse * rows
    half = rows // 2
    r = np.arange(rows)[None, :]
    k = np.arange(half)[:, None]

    def pair(j):
        angle = 2.0 * np.pi * ((r * (coarse * k + j)) % total) / total
        return np.cos(angle), np.sin(angle)

    tables = np.zeros((parts, 2 * rows, 2 * rows), np.float32)
    cos0, sin0 = pair(0)
    cosn, sinn = pair(parts)
    tables[0, :half, :rows] = cos0
    tables[0, half:rows, :rows] = -sin0
    tables[0, rows : rows + half, rows:] = cosn
    tables[0, rows + half :, rows:] = -sinn
    for m in range(1, parts):
        c, s = pair(m)
        tables[m, :rows] = np.block([[c, s], [-s, c]])
        c, s = pair(coarse - m)
        tables[m, rows:] = np.block([[c, -s], [-s, -c]])
    return tables.astype(jnp.bfloat16)


def regroup_matrix(count, coarse):
    fine = count // coarse
    matrix = np.zeros((count, count), np.float32)
    out = np.arange(count)
    matrix[out, (out % fine) * coarse + out // fine] = 1.0
    return matrix.astype(jnp.bfloat16)


def weighted(terms):
    total = None
    for weight, value in terms:
        if abs(weight) < 1e-12:
            continue
        if abs(weight - 1.0) < 1e-12:
            part = value
        elif abs(weight + 1.0) < 1e-12:
            part = -value
        else:
            part = value * weight
        total = part if total is None else total + part
    return total


def layer_kernel(
    parts, pieces,
    proj_hbm, taps_ref, skip_ref, filt_hbm, weight_hbm, tables_hbm, regroup_ref,
    out_ref,
    proj, filt, weight, tables, rim,
    query, signal, signal_bf, heard, filt_bf, resp,
    coarse_in, spectrum, inverse, narrow_out, returned, gated,
    side_out, side_in, far_out, far_in, side_own_out, side_own_in,
    load_sem, rim_sem, sig_send, sig_recv, filt_send, filt_recv,
    back_send, back_recv, side_send, side_recv, far_send, far_recv, own_send, own_recv,
):
    seq = lax.axis_index("seq")
    chan = lax.axis_index("chan")
    groups = parts // 2
    half = seq // groups
    group = seq % groups
    sibling = chan + 1 - 2 * (chan % 2)
    across = (chan + 2) % 4
    diagonal = (sibling + 2) % 4
    rows = proj.shape[1]
    coarse = 2 * parts
    half_rows = rows // 2
    fine_held = filt.shape[1] // coarse
    out_width = out_ref.shape[1]
    piece = out_width // pieces

    load_proj = pltpu.make_async_copy(proj_hbm, proj, load_sem.at[0])
    load_proj.start()
    load_filt = []
    for p in range(2):
        load_filt.append(pltpu.make_async_copy(filt_hbm.at[p], filt.at[p], load_sem.at[1 + p]))
        load_filt[-1].start()
    load_tables = pltpu.make_async_copy(tables_hbm, tables, load_sem.at[3])
    load_tables.start()
    load_weight = pltpu.make_async_copy(weight_hbm, weight, load_sem.at[4])
    load_weight.start()

    barrier = pltpu.get_barrier_semaphore()
    for o in range(1, parts):
        pl.semaphore_signal(barrier, inc=1, device_id={"seq": (seq + o) % parts}, device_id_type=MESH)
    for partner in (sibling, across):
        pl.semaphore_signal(barrier, inc=1, device_id={"chan": partner}, device_id_type=MESH)
    pl.semaphore_wait(barrier, parts + 1)

    load_proj.wait()
    rim_copy = pltpu.make_async_remote_copy(
        src_ref=proj.at[:, pl.ds(rows - 16, 16), :],
        dst_ref=rim,
        send_sem=rim_sem.at[0],
        recv_sem=rim_sem.at[1],
        device_id={"seq": (seq + 1) % parts},
        device_id_type=MESH,
    )
    rim_copy.start()

    filt_copies = []

    def send_filter(p):
        load_filt[p].wait()
        filt_bf[p] = jnp.dot(
            regroup_ref[...], filt[p].astype(jnp.bfloat16), preferred_element_type=jnp.float32
        ).astype(jnp.bfloat16)
        for o in range(1, groups):
            target = (group + o) % groups
            columns = pl.ds(pl.multiple_of(target * LANES, LANES), LANES)
            copy = pltpu.make_async_remote_copy(
                src_ref=filt_bf.at[p, :, columns],
                dst_ref=resp.at[group, p],
                send_sem=filt_send.at[p, o],
                recv_sem=filt_recv.at[p, o],
                device_id={"seq": half * groups + target},
                device_id_type=MESH,
            )
            copy.start()
            filt_copies.append(copy)

    send_filter(0)
    rim_copy.wait()

    row_index = lax.broadcasted_iota(jnp.int32, (rows, LANES), 0)

    def shaped(i, columns):
        now = proj[i, :, columns].astype(jnp.float32)
        edge = rim[i, :, columns].astype(jnp.float32)
        edge = jnp.where(seq == 0, jnp.zeros_like(edge), edge)
        last, before = edge[15:16], edge[14:15]
        one = jnp.where(row_index == 0, last, pltpu.roll(now, 1, 0))
        two = jnp.where(row_index == 0, before, jnp.where(row_index == 1, last, pltpu.roll(now, 2, 0)))
        return (
            taps_ref[3 * i : 3 * i + 1, columns] * now
            + taps_ref[3 * i + 1 : 3 * i + 2, columns] * one
            + taps_ref[3 * i + 2 : 3 * i + 3, columns] * two
        )

    for g in range(groups):
        columns = slice(g * LANES, (g + 1) * LANES)
        product = shaped(1, columns) * shaped(2, columns)
        signal[:, columns] = product
        signal_bf[:, columns] = product.astype(jnp.bfloat16)

    own_columns = pl.ds(pl.multiple_of(group * LANES, LANES), LANES)
    sig_copies = []
    for o in range(1, parts):
        target = (seq + o) % parts
        columns = pl.ds(pl.multiple_of((target % groups) * LANES, LANES), LANES)
        copy = pltpu.make_async_remote_copy(
            src_ref=signal_bf.at[:, columns],
            dst_ref=heard.at[seq],
            send_sem=sig_send.at[o],
            recv_sem=sig_recv.at[o],
            device_id={"seq": target},
            device_id_type=MESH,
        )
        copy.start()
        sig_copies.append(copy)
    heard[seq] = signal_bf[:, own_columns]
    send_filter(1)
    for p in range(2):
        resp[group, p] = filt_bf[p, :, own_columns]
    for g in range(groups):
        columns = slice(g * LANES, (g + 1) * LANES)
        query[:, columns] = shaped(0, columns)

    for copy in sig_copies:
        copy.wait_recv()

    chunk = 32

    def parity(start):
        index = lax.broadcasted_iota(jnp.int32, (chunk, LANES), 0)
        return (1 - 2 * half * (index % 2)).astype(jnp.float32)

    angle = 2.0 * math.pi / coarse

    def forward(step, carry):
        start = pl.multiple_of(step * chunk, chunk)
        sign = parity(start)
        x = [heard[n, pl.ds(start, chunk), :].astype(jnp.float32) * sign for n in range(parts)]
        for m in range(parts):
            if m == 0:
                real = weighted([(1.0, x[n]) for n in range(parts)])
                imag = weighted([((-1.0) ** n, x[n]) for n in range(parts)])
            else:
                real = weighted([(math.cos(angle * m * n), x[n]) for n in range(parts)])
                imag = weighted([(-math.sin(angle * m * n), x[n]) for n in range(parts)])
            coarse_in[m, pl.ds(start, chunk), :] = real.astype(jnp.bfloat16)
            coarse_in[m, pl.ds(rows + start, chunk), :] = imag.astype(jnp.bfloat16)
        return carry

    lax.fori_loop(0, rows // chunk, forward, 0)
    load_tables.wait()
    for m in range(parts):
        spectrum[m] = jnp.dot(tables[m], coarse_in[m], preferred_element_type=jnp.float32)

    for copy in filt_copies:
        copy.wait_recv()

    for m in range(parts):
        kept = []
        for at, j in ((0, m), (rows, parts if m == 0 else coarse - m)):
            real = spectrum[m, at : at + half_rows]
            imag = spectrum[m, at + half_rows : at + rows]
            held = slice(j * fine_held, (j + 1) * fine_held)
            resp_real = jnp.concatenate([resp[g, 0, held] for g in range(groups)], 0).astype(jnp.float32)
            resp_imag = jnp.concatenate([resp[g, 1, held] for g in range(groups)], 0).astype(jnp.float32)
            kept.append((real * resp_real - imag * resp_imag).astype(jnp.bfloat16))
            kept.append((real * resp_imag + imag * resp_real).astype(jnp.bfloat16))
        inverse[m] = lax.dot_general(
            tables[m], jnp.concatenate(kept, 0), (((0,), (0,)), ((), ())), preferred_element_type=jnp.float32
        )

    def backward(step, carry):
        start = pl.multiple_of(step * chunk, chunk)
        sign = parity(start) * (1.0 / (coarse * rows))
        real = [inverse[m, pl.ds(start, chunk), :] for m in range(parts)]
        imag = [inverse[m, pl.ds(rows + start, chunk), :] for m in range(parts)]
        for n in range(parts):
            terms = [(1.0, real[0]), ((-1.0) ** n, imag[0])]
            for m in range(1, parts):
                terms.append((math.cos(angle * m * n), real[m]))
                terms.append((-math.sin(angle * m * n), imag[m]))
            narrow_out[n, pl.ds(start, chunk), :] = (weighted(terms) * sign).astype(jnp.bfloat16)
        return carry

    lax.fori_loop(0, rows // chunk, backward, 0)
    back_copies = []
    for o in range(1, parts):
        target = (seq + o) % parts
        copy = pltpu.make_async_remote_copy(
            src_ref=narrow_out.at[target],
            dst_ref=returned.at[seq],
            send_sem=back_send.at[o],
            recv_sem=back_recv.at[o],
            device_id={"seq": target},
            device_id_type=MESH,
        )
        copy.start()
        back_copies.append(copy)
    returned[seq] = narrow_out[seq]
    load_weight.wait()
    for copy in back_copies:
        copy.wait_recv()

    for g in range(groups):
        columns = slice(g * LANES, (g + 1) * LANES)
        filtered = returned[g].astype(jnp.float32) + returned[groups + g].astype(jnp.float32)
        gated[:, columns] = (
            query[:, columns] * (filtered + skip_ref[:, columns] * signal[:, columns])
        ).astype(jnp.bfloat16)

    def product(block, c):
        columns = pl.ds(pl.multiple_of(block * out_width + c * piece, piece), piece)
        return jnp.dot(gated[...], weight[:, columns], preferred_element_type=jnp.float32)

    def send(source, target_ref, send_sem, recv_sem, c, partner):
        copy = pltpu.make_async_remote_copy(
            src_ref=source.at[c],
            dst_ref=target_ref.at[c],
            send_sem=send_sem.at[c],
            recv_sem=recv_sem.at[c],
            device_id={"chan": partner},
            device_id_type=MESH,
        )
        copy.start()
        return copy

    side_copies, far_copies, own_copies = [], [], []
    for c in range(pieces):
        side_out[c] = product(diagonal, c).astype(jnp.bfloat16)
        side_copies.append(send(side_out, side_in, side_send, side_recv, c, sibling))
    for c in range(pieces):
        mine = product(across, c)
        side_copies[c].wait_recv()
        far_out[c] = (mine + side_in[c].astype(jnp.float32)).astype(jnp.bfloat16)
        far_copies.append(send(far_out, far_in, far_send, far_recv, c, across))
    for c in range(pieces):
        side_own_out[c] = product(sibling, c).astype(jnp.bfloat16)
        own_copies.append(send(side_own_out, side_own_in, own_send, own_recv, c, sibling))
    for c in range(pieces):
        mine = product(chan, c)
        own_copies[c].wait_recv()
        far_copies[c].wait_recv()
        out_ref[:, c * piece : (c + 1) * piece] = (
            mine + side_own_in[c].astype(jnp.float32) + far_in[c].astype(jnp.float32)
        ).astype(jnp.bfloat16)
    for copy in filt_copies + sig_copies + back_copies + side_copies + far_copies + own_copies:
        copy.wait_send()


def per_device_kernel(projected, short_taps, skip_gain, filter_response, out_weight):
    parts = lax.axis_size("seq")
    chans = lax.axis_size("chan")
    rows, width = projected.shape[1:]
    held = filter_response.shape[1]
    out_width = out_weight.shape[1] // chans
    groups = parts // 2
    pieces = 4
    piece = out_width // pieces
    bf, f32 = jnp.bfloat16, jnp.float32
    any_spec = pl.BlockSpec(memory_space=pl.ANY)
    vmem_spec = pl.BlockSpec(memory_space=pltpu.VMEM)
    dma = pltpu.SemaphoreType.DMA
    exchange = pltpu.VMEM((pieces, rows, piece), bf)
    return pl.pallas_call(
        functools.partial(layer_kernel, parts, pieces),
        out_shape=jax.ShapeDtypeStruct((rows, out_width), bf),
        in_specs=[any_spec, vmem_spec, vmem_spec, any_spec, any_spec, any_spec, vmem_spec],
        out_specs=vmem_spec,
        scratch_shapes=[
            pltpu.VMEM((3, rows, width), bf),
            pltpu.VMEM((2, held, width), f32),
            pltpu.VMEM(out_weight.shape, bf),
            pltpu.VMEM((parts, 2 * rows, 2 * rows), bf),
            pltpu.VMEM((3, 16, width), bf),
            pltpu.VMEM((rows, width), f32),
            pltpu.VMEM((rows, width), f32),
            pltpu.VMEM((rows, width), bf),
            pltpu.VMEM((parts, rows, LANES), bf),
            pltpu.VMEM((2, held, width), bf),
            pltpu.VMEM((groups, 2, held, LANES), bf),
            pltpu.VMEM((parts, 2 * rows, LANES), bf),
            pltpu.VMEM((parts, 2 * rows, LANES), f32),
            pltpu.VMEM((parts, 2 * rows, LANES), f32),
            pltpu.VMEM((parts, rows, LANES), bf),
            pltpu.VMEM((parts, rows, LANES), bf),
            pltpu.VMEM((rows, width), bf),
            exchange, exchange, exchange, exchange, exchange, exchange,
            dma((5,)), dma((2,)),
            dma((parts,)), dma((parts,)),
            dma((2, groups)), dma((2, groups)),
            dma((parts,)), dma((parts,)),
            dma((pieces,)), dma((pieces,)),
            dma((pieces,)), dma((pieces,)),
            dma((pieces,)), dma((pieces,)),
        ],
        compiler_params=pltpu.CompilerParams(
            collective_id=0, has_side_effects=True, vmem_limit_bytes=56 * 1024 * 1024
        ),
    )(
        projected,
        short_taps.reshape(9, width),
        skip_gain.reshape(1, width),
        filter_response,
        out_weight,
        jnp.asarray(dft_tables(rows, parts)),
        jnp.asarray(regroup_matrix(held, 2 * parts)),
    )


def shifted(value, axis, steps):
    count = lax.axis_size(axis)
    first, last = (max(0, -steps), min(count, count - steps))
    return lax.ppermute(value, axis, [(source, source + steps) for source in range(first, last)])


def product_einsum(form, left, right):
    return jnp.einsum(form, left, right, precision=lax.Precision.HIGHEST)


def per_device_collectives(projected, short_taps, skip_gain, filter_response, out_weight):
    seq_rows = projected.shape[1]
    seq_parts = lax.axis_size("seq")
    coarse_len = 2 * seq_parts
    total_len = coarse_len * seq_rows
    rim_rows = shifted(projected[:, seq_rows - 2 :, :], "seq", 1)
    padded = jnp.concatenate([rim_rows, projected], axis=1).astype(jnp.float32)
    shaped = (
        short_taps[:, 0, None, :] * padded[:, 2:]
        + short_taps[:, 1, None, :] * padded[:, 1:-1]
        + short_taps[:, 2, None, :] * padded[:, :-2]
    )
    query = shaped[0]
    signal = shaped[1] * shaped[2]
    coarse_freq = jnp.arange(coarse_len, dtype=jnp.int32)
    coarse_pos = jnp.arange(seq_parts, dtype=jnp.int32)
    coarse_angle = (
        2.0
        * math.pi
        / coarse_len
        * (coarse_freq[:, None] * coarse_pos[None, :] % coarse_len).astype(jnp.float32)
    )
    coarse_cos = jnp.cos(coarse_angle)
    coarse_sin = jnp.sin(coarse_angle)
    fine_index = jnp.arange(seq_rows, dtype=jnp.int32)
    fine_angle = (
        2.0
        * math.pi
        / seq_rows
        * (fine_index[:, None] * fine_index[None, :] % seq_rows).astype(jnp.float32)
    )
    fine_cos = jnp.cos(fine_angle)
    fine_sin = jnp.sin(fine_angle)
    narrow = lax.all_to_all(
        signal.astype(jnp.bfloat16), "seq", split_axis=1, concat_axis=0, tiled=True
    ).astype(signal.dtype)
    resp_narrow = lax.all_to_all(
        filter_response.astype(jnp.bfloat16), "seq", split_axis=2, concat_axis=1, tiled=True
    ).astype(filter_response.dtype)
    narrow_width = narrow.shape[1]
    blocks = narrow.reshape(seq_parts, seq_rows, narrow_width)
    whole_angle = (
        2.0
        * math.pi
        / total_len
        * (coarse_freq[:, None] * fine_index[None, :] % total_len).astype(jnp.float32)
    )
    whole_cos = jnp.cos(whole_angle)[:, :, None]
    whole_sin = jnp.sin(whole_angle)[:, :, None]
    first_real = product_einsum("kn,nrc->krc", coarse_cos, blocks)
    first_imag = -product_einsum("kn,nrc->krc", coarse_sin, blocks)
    turned_real = first_real * whole_cos + first_imag * whole_sin
    turned_imag = first_imag * whole_cos - first_real * whole_sin
    spec_real = product_einsum("kn,jnc->kjc", fine_cos, turned_real) + product_einsum(
        "kn,jnc->kjc", fine_sin, turned_imag
    )
    spec_imag = product_einsum("kn,jnc->kjc", fine_cos, turned_imag) - product_einsum(
        "kn,jnc->kjc", fine_sin, turned_real
    )
    resp_grid = resp_narrow.reshape(2, seq_rows, coarse_len, narrow_width)
    kept_real = spec_real * resp_grid[0] - spec_imag * resp_grid[1]
    kept_imag = spec_real * resp_grid[1] + spec_imag * resp_grid[0]
    back_real = product_einsum("kn,kjc->jnc", fine_cos, kept_real) - product_einsum(
        "kn,kjc->jnc", fine_sin, kept_imag
    )
    back_imag = product_einsum("kn,kjc->jnc", fine_cos, kept_imag) + product_einsum(
        "kn,kjc->jnc", fine_sin, kept_real
    )
    untwist_real = back_real * whole_cos - back_imag * whole_sin
    untwist_imag = back_real * whole_sin + back_imag * whole_cos
    inverse_part = (
        product_einsum("kn,krc->nrc", coarse_cos, untwist_real)
        - product_einsum("kn,krc->nrc", coarse_sin, untwist_imag)
    ) * (1.0 / total_len)
    filtered = lax.all_to_all(
        inverse_part.reshape(seq_parts * seq_rows, narrow_width).astype(jnp.bfloat16),
        "seq",
        split_axis=0,
        concat_axis=1,
        tiled=True,
    ).astype(jnp.float32)
    gated = (query * (filtered + skip_gain[None, :] * signal)).astype(jnp.bfloat16)
    partial_terms = jnp.dot(gated, out_weight, preferred_element_type=jnp.float32)
    return lax.psum_scatter(
        partial_terms.astype(jnp.bfloat16), "chan", scatter_dimension=1, tiled=True
    )


def per_device(projected, short_taps, skip_gain, filter_response, out_weight):
    parts = lax.axis_size("seq")
    rows, width = projected.shape[1:]
    fits = (
        parts == 8
        and lax.axis_size("chan") == 4
        and width == parts // 2 * LANES
        and rows % 32 == 0
        and filter_response.shape[1] == 2 * rows
        and out_weight.shape[1] % (16 * LANES) == 0
    )
    form = per_device_kernel if fits else per_device_collectives
    return form(projected, short_taps, skip_gain, filter_response, out_weight)


def solution(mesh):
    placed = (
        P(None, "seq", "chan"),
        P(None, None, "chan"),
        P("chan"),
        P(None, "seq", "chan"),
        P("chan", None),
    )
    return jax.shard_map(
        per_device, mesh=mesh, in_specs=placed, out_specs=P("seq", "chan"), check_vma=False
    )
```

```python
import functools
import math

import jax
import jax.numpy as jnp
import numpy as np
from jax import lax
from jax.experimental import pallas as pl
from jax.experimental.pallas import tpu as pltpu
from jax.sharding import PartitionSpec as P

LANES = 128
MESH = pl.DeviceIdType.MESH


def dft_tables(rows, parts):
    coarse = 2 * parts
    total = coarse * rows
    half = rows // 2
    r = np.arange(rows)[None, :]
    k = np.arange(half)[:, None]

    def pair(j):
        angle = 2.0 * np.pi * ((r * (coarse * k + j)) % total) / total
        return np.cos(angle), np.sin(angle)

    tables = np.zeros((parts, 2 * rows, 2 * rows), np.float32)
    cos0, sin0 = pair(0)
    cosn, sinn = pair(parts)
    tables[0, :half, :rows] = cos0
    tables[0, half:rows, :rows] = -sin0
    tables[0, rows : rows + half, rows:] = cosn
    tables[0, rows + half :, rows:] = -sinn
    for m in range(1, parts):
        c, s = pair(m)
        tables[m, :rows] = np.block([[c, s], [-s, c]])
        c, s = pair(coarse - m)
        tables[m, rows:] = np.block([[c, -s], [-s, -c]])
    return tables.astype(jnp.bfloat16)


def regroup_matrix(count, coarse):
    fine = count // coarse
    matrix = np.zeros((count, count), np.float32)
    out = np.arange(count)
    matrix[out, (out % fine) * coarse + out // fine] = 1.0
    return matrix.astype(jnp.bfloat16)


def weighted(terms):
    total = None
    for weight, value in terms:
        if abs(weight) < 1e-12:
            continue
        if abs(weight - 1.0) < 1e-12:
            part = value
        elif abs(weight + 1.0) < 1e-12:
            part = -value
        else:
            part = value * weight
        total = part if total is None else total + part
    return total


def layer_kernel(
    parts, pieces, row_chunks,
    proj_hbm, taps_ref, skip_ref, filt_hbm, weight_hbm, tables_hbm, regroup_hbm,
    out_ref,
    proj, filt, weight, tables, regroup, rim,
    query, signal, signal_bf, heard, filt_bf, resp,
    coarse_in, spectrum, inverse, narrow_out, returned, gated,
    side_out, side_in, far_out, far_in, side_own_out, side_own_in, own_sum,
    load_sem, rim_sem, sig_send, sig_recv, filt_send, filt_recv,
    back_send, back_recv, side_sems, far_sems, own_sems,
):
    seq = lax.axis_index("seq")
    chan = lax.axis_index("chan")
    groups = parts // 2
    half = seq // groups
    group = seq % groups
    sibling = chan + 1 - 2 * (chan % 2)
    across = (chan + 2) % 4
    diagonal = (sibling + 2) % 4
    rows = proj.shape[1]
    coarse = 2 * parts
    half_rows = rows // 2
    fine_held = filt.shape[1] // coarse
    out_width = out_ref.shape[1]
    piece = out_width // pieces

    barrier = pltpu.get_barrier_semaphore()
    for o in range(1, parts):
        pl.semaphore_signal(barrier, inc=1, device_id={"seq": (seq + o) % parts}, device_id_type=MESH)
    for partner in (sibling, across):
        pl.semaphore_signal(barrier, inc=1, device_id={"chan": partner}, device_id_type=MESH)

    load_proj = pltpu.make_async_copy(proj_hbm, proj, load_sem.at[0])
    load_proj.start()
    load_regroup = pltpu.make_async_copy(regroup_hbm, regroup, load_sem.at[5])
    load_regroup.start()
    load_filt = []
    for p in range(2):
        load_filt.append(pltpu.make_async_copy(filt_hbm.at[p], filt.at[p], load_sem.at[1 + p]))
        load_filt[-1].start()
    load_tables = pltpu.make_async_copy(tables_hbm, tables, load_sem.at[3])
    load_weight = pltpu.make_async_copy(weight_hbm, weight, load_sem.at[4])

    load_proj.wait()
    pl.semaphore_wait(barrier, parts + 1)
    rim_copy = pltpu.make_async_remote_copy(
        src_ref=proj.at[:, pl.ds(rows - 16, 16), :],
        dst_ref=rim,
        send_sem=rim_sem.at[0],
        recv_sem=rim_sem.at[1],
        device_id={"seq": (seq + 1) % parts},
        device_id_type=MESH,
    )
    rim_copy.start()

    filt_copies = []

    def send_filter(p):
        load_filt[p].wait()
        filt_bf[p] = jnp.dot(
            regroup[...], filt[p].astype(jnp.bfloat16), preferred_element_type=jnp.float32
        ).astype(jnp.bfloat16)
        for o in range(1, groups):
            target = (group + o) % groups
            columns = pl.ds(pl.multiple_of(target * LANES, LANES), LANES)
            copy = pltpu.make_async_remote_copy(
                src_ref=filt_bf.at[p, :, columns],
                dst_ref=resp.at[group, p],
                send_sem=filt_send.at[p, o],
                recv_sem=filt_recv.at[p, o],
                device_id={"seq": half * groups + target},
                device_id_type=MESH,
            )
            copy.start()
            filt_copies.append(copy)

    def shaped(i, columns, count, fixed):
        now = proj[i, :count, columns].astype(jnp.float32)
        one, two = pltpu.roll(now, 1, 0), pltpu.roll(now, 2, 0)
        if fixed:
            row_index = lax.broadcasted_iota(jnp.int32, now.shape, 0)
            edge = rim[i, :, columns].astype(jnp.float32)
            edge = jnp.where(seq == 0, jnp.zeros_like(edge), edge)
            last, before = edge[15:16], edge[14:15]
            one = jnp.where(row_index == 0, last, one)
            two = jnp.where(row_index == 0, before, jnp.where(row_index == 1, last, two))
        return (
            taps_ref[i, 0:1, columns] * now
            + taps_ref[i, 1:2, columns] * one
            + taps_ref[i, 2:3, columns] * two
        )

    def shape_signal(count, fixed):
        for g in range(groups):
            columns = slice(g * LANES, (g + 1) * LANES)
            value = shaped(1, columns, count, fixed) * shaped(2, columns, count, fixed)
            signal[:count, columns] = value
            signal_bf[:count, columns] = value.astype(jnp.bfloat16)

    def shape_query(count, fixed):
        for g in range(groups):
            columns = slice(g * LANES, (g + 1) * LANES)
            query[:count, columns] = shaped(0, columns, count, fixed)

    shape_signal(rows, False)
    load_regroup.wait()
    send_filter(0)
    rim_copy.wait()
    shape_signal(16, True)

    own_columns = pl.ds(pl.multiple_of(group * LANES, LANES), LANES)
    sig_copies = []
    for o in sorted(range(1, parts), key=lambda o: abs(o - groups)):
        target = (seq + o) % parts
        columns = pl.ds(pl.multiple_of((target % groups) * LANES, LANES), LANES)
        copy = pltpu.make_async_remote_copy(
            src_ref=signal_bf.at[:, columns],
            dst_ref=heard.at[seq],
            send_sem=sig_send.at[o],
            recv_sem=sig_recv.at[o],
            device_id={"seq": target},
            device_id_type=MESH,
        )
        copy.start()
        sig_copies.append(copy)
    heard[seq] = signal_bf[:, own_columns]
    send_filter(1)
    load_tables.start()
    load_weight.start()
    for p in range(2):
        resp[group, p] = filt_bf[p, :, own_columns]
    shape_query(rows, False)
    shape_query(16, True)

    for copy in sig_copies:
        copy.wait_recv()

    chunk = 32

    def parity(start):
        index = lax.broadcasted_iota(jnp.int32, (chunk, LANES), 0)
        return (1 - 2 * half * (index % 2)).astype(jnp.float32)

    angle = 2.0 * math.pi / coarse

    def forward(step, carry):
        start = pl.multiple_of(step * chunk, chunk)
        sign = parity(start)
        x = [heard[n, pl.ds(start, chunk), :].astype(jnp.float32) * sign for n in range(parts)]
        for m in range(parts):
            if m == 0:
                real = weighted([(1.0, x[n]) for n in range(parts)])
                imag = weighted([((-1.0) ** n, x[n]) for n in range(parts)])
            else:
                real = weighted([(math.cos(angle * m * n), x[n]) for n in range(parts)])
                imag = weighted([(-math.sin(angle * m * n), x[n]) for n in range(parts)])
            coarse_in[m, pl.ds(start, chunk), :] = real.astype(jnp.bfloat16)
            coarse_in[m, pl.ds(rows + start, chunk), :] = imag.astype(jnp.bfloat16)
        return carry

    lax.fori_loop(0, rows // chunk, forward, 0)
    load_tables.wait()
    for m in range(parts):
        spectrum[m] = jnp.dot(tables[m], coarse_in[m], preferred_element_type=jnp.float32)

    for copy in filt_copies:
        copy.wait_recv()

    for m in range(parts):
        kept = []
        for at, j in ((0, m), (rows, parts if m == 0 else coarse - m)):
            real = spectrum[m, at : at + half_rows]
            imag = spectrum[m, at + half_rows : at + rows]
            held = slice(j * fine_held, (j + 1) * fine_held)
            resp_real = jnp.concatenate([resp[g, 0, held] for g in range(groups)], 0).astype(jnp.float32)
            resp_imag = jnp.concatenate([resp[g, 1, held] for g in range(groups)], 0).astype(jnp.float32)
            kept.append((real * resp_real - imag * resp_imag).astype(jnp.bfloat16))
            kept.append((real * resp_imag + imag * resp_real).astype(jnp.bfloat16))
        inverse[m] = lax.dot_general(
            tables[m], jnp.concatenate(kept, 0), (((0,), (0,)), ((), ())), preferred_element_type=jnp.float32
        )

    def backward(step, carry):
        start = pl.multiple_of(step * chunk, chunk)
        sign = parity(start) * (1.0 / (coarse * rows))
        real = [inverse[m, pl.ds(start, chunk), :] for m in range(parts)]
        imag = [inverse[m, pl.ds(rows + start, chunk), :] for m in range(parts)]
        for n in range(parts):
            terms = [(1.0, real[0]), ((-1.0) ** n, imag[0])]
            for m in range(1, parts):
                terms.append((math.cos(angle * m * n), real[m]))
                terms.append((-math.sin(angle * m * n), imag[m]))
            narrow_out[n, pl.ds(start, chunk), :] = (weighted(terms) * sign).astype(jnp.bfloat16)
        return carry

    back_copies = []
    for t, (first, count) in enumerate(row_chunks):
        lax.fori_loop(first // chunk, (first + count) // chunk, backward, 0)
        here = pl.ds(first, count)
        back_copies.append([])
        for o in sorted(range(1, parts), key=lambda o: abs(o - groups)):
            target = (seq + o) % parts
            copy = pltpu.make_async_remote_copy(
                src_ref=narrow_out.at[target, here],
                dst_ref=returned.at[seq, here],
                send_sem=back_send.at[t, o],
                recv_sem=back_recv.at[t, o],
                device_id={"seq": target},
                device_id_type=MESH,
            )
            copy.start()
            back_copies[t].append(copy)
    returned[seq] = narrow_out[seq]
    load_weight.wait()

    def send(source, target_ref, sems, at, part, partner):
        rows_at, columns = part
        copy = pltpu.make_async_remote_copy(
            src_ref=source.at[rows_at, columns],
            dst_ref=target_ref.at[rows_at, columns],
            send_sem=sems.at[0, at],
            recv_sem=sems.at[1, at],
            device_id={"chan": partner},
            device_id_type=MESH,
        )
        copy.start()
        return copy

    side_copies, far_copies, own_copies, all_parts = [], [], [], []
    for t, (first, count) in enumerate(row_chunks):
        for copy in back_copies[t]:
            copy.wait_recv()
        here = slice(first, first + count)
        for g in range(groups):
            columns = slice(g * LANES, (g + 1) * LANES)
            filtered = returned[g, here].astype(jnp.float32) + returned[groups + g, here].astype(jnp.float32)
            gated[here, columns] = (
                query[here, columns] * (filtered + skip_ref[:, columns] * signal[here, columns])
            ).astype(jnp.bfloat16)

        def product(block, c):
            columns = pl.ds(pl.multiple_of(block * out_width + c * piece, piece), piece)
            return jnp.dot(gated[here], weight[:, columns], preferred_element_type=jnp.float32)

        base = len(all_parts)
        parts_here = [(pl.ds(first, count), pl.ds(c * piece, piece)) for c in range(pieces)]
        all_parts += parts_here
        for c, part in enumerate(parts_here):
            side_out[part] = product(diagonal, c).astype(jnp.bfloat16)
            side_copies.append(send(side_out, side_in, side_sems, base + c, part, sibling))
        for c, part in enumerate(parts_here):
            mine = product(across, c)
            side_copies[base + c].wait_recv()
            far_out[part] = (mine + side_in[part].astype(jnp.float32)).astype(jnp.bfloat16)
            far_copies.append(send(far_out, far_in, far_sems, base + c, part, across))
        for c, part in enumerate(parts_here):
            side_own_out[part] = product(sibling, c).astype(jnp.bfloat16)
            own_copies.append(send(side_own_out, side_own_in, own_sems, base + c, part, sibling))
        for c, part in enumerate(parts_here):
            own_sum[part] = product(chan, c)
    for at, part in enumerate(all_parts):
        own_copies[at].wait_recv()
        far_copies[at].wait_recv()
        out_ref[part] = (
            own_sum[part] + side_own_in[part].astype(jnp.float32) + far_in[part].astype(jnp.float32)
        ).astype(jnp.bfloat16)
    for copy in filt_copies + sig_copies + sum(back_copies, []) + side_copies + far_copies + own_copies:
        copy.wait_send()


def per_device_kernel(projected, short_taps, skip_gain, filter_response, out_weight):
    parts = lax.axis_size("seq")
    chans = lax.axis_size("chan")
    rows, width = projected.shape[1:]
    held = filter_response.shape[1]
    out_width = out_weight.shape[1] // chans
    groups = parts // 2
    pieces = 2
    quarter = rows // 4
    row_chunks = ((0, quarter), (quarter, quarter), (2 * quarter, 2 * quarter))
    count = pieces * len(row_chunks)
    bf, f32 = jnp.bfloat16, jnp.float32
    any_spec = pl.BlockSpec(memory_space=pl.ANY)
    vmem_spec = pl.BlockSpec(memory_space=pltpu.VMEM)
    dma = pltpu.SemaphoreType.DMA
    exchange = pltpu.VMEM((rows, out_width), bf)
    return pl.pallas_call(
        functools.partial(layer_kernel, parts, pieces, row_chunks),
        out_shape=jax.ShapeDtypeStruct((rows, out_width), bf),
        in_specs=[any_spec, vmem_spec, vmem_spec, any_spec, any_spec, any_spec, any_spec],
        out_specs=vmem_spec,
        scratch_shapes=[
            pltpu.VMEM((3, rows, width), bf),
            pltpu.VMEM((2, held, width), f32),
            pltpu.VMEM(out_weight.shape, bf),
            pltpu.VMEM((parts, 2 * rows, 2 * rows), bf),
            pltpu.VMEM((held, held), bf),
            pltpu.VMEM((3, 16, width), bf),
            pltpu.VMEM((rows, width), f32),
            pltpu.VMEM((rows, width), f32),
            pltpu.VMEM((rows, width), bf),
            pltpu.VMEM((parts, rows, LANES), bf),
            pltpu.VMEM((2, held, width), bf),
            pltpu.VMEM((groups, 2, held, LANES), bf),
            pltpu.VMEM((parts, 2 * rows, LANES), bf),
            pltpu.VMEM((parts, 2 * rows, LANES), f32),
            pltpu.VMEM((parts, 2 * rows, LANES), f32),
            pltpu.VMEM((parts, rows, LANES), bf),
            pltpu.VMEM((parts, rows, LANES), bf),
            pltpu.VMEM((rows, width), bf),
            exchange, exchange, exchange, exchange, exchange, exchange,
            pltpu.VMEM((rows, out_width), f32),
            dma((6,)), dma((2,)),
            dma((parts,)), dma((parts,)),
            dma((2, groups)), dma((2, groups)),
            dma((len(row_chunks), parts)), dma((len(row_chunks), parts)),
            dma((2, count)), dma((2, count)), dma((2, count)),
        ],
        compiler_params=pltpu.CompilerParams(
            collective_id=0, has_side_effects=True, vmem_limit_bytes=56 * 1024 * 1024
        ),
    )(
        projected,
        short_taps,
        skip_gain.reshape(1, width),
        filter_response,
        out_weight,
        jnp.asarray(dft_tables(rows, parts)),
        jnp.asarray(regroup_matrix(held, 2 * parts)),
    )


def shifted(value, axis, steps):
    count = lax.axis_size(axis)
    first, last = (max(0, -steps), min(count, count - steps))
    return lax.ppermute(value, axis, [(source, source + steps) for source in range(first, last)])


def product_einsum(form, left, right):
    return jnp.einsum(form, left, right, precision=lax.Precision.HIGHEST)


def per_device_collectives(projected, short_taps, skip_gain, filter_response, out_weight):
    seq_rows = projected.shape[1]
    seq_parts = lax.axis_size("seq")
    coarse_len = 2 * seq_parts
    total_len = coarse_len * seq_rows
    rim_rows = shifted(projected[:, seq_rows - 2 :, :], "seq", 1)
    padded = jnp.concatenate([rim_rows, projected], axis=1).astype(jnp.float32)
    shaped = (
        short_taps[:, 0, None, :] * padded[:, 2:]
        + short_taps[:, 1, None, :] * padded[:, 1:-1]
        + short_taps[:, 2, None, :] * padded[:, :-2]
    )
    query = shaped[0]
    signal = shaped[1] * shaped[2]
    coarse_freq = jnp.arange(coarse_len, dtype=jnp.int32)
    coarse_pos = jnp.arange(seq_parts, dtype=jnp.int32)
    coarse_angle = (
        2.0
        * math.pi
        / coarse_len
        * (coarse_freq[:, None] * coarse_pos[None, :] % coarse_len).astype(jnp.float32)
    )
    coarse_cos = jnp.cos(coarse_angle)
    coarse_sin = jnp.sin(coarse_angle)
    fine_index = jnp.arange(seq_rows, dtype=jnp.int32)
    fine_angle = (
        2.0
        * math.pi
        / seq_rows
        * (fine_index[:, None] * fine_index[None, :] % seq_rows).astype(jnp.float32)
    )
    fine_cos = jnp.cos(fine_angle)
    fine_sin = jnp.sin(fine_angle)
    narrow = lax.all_to_all(
        signal.astype(jnp.bfloat16), "seq", split_axis=1, concat_axis=0, tiled=True
    ).astype(signal.dtype)
    resp_narrow = lax.all_to_all(
        filter_response.astype(jnp.bfloat16), "seq", split_axis=2, concat_axis=1, tiled=True
    ).astype(filter_response.dtype)
    narrow_width = narrow.shape[1]
    blocks = narrow.reshape(seq_parts, seq_rows, narrow_width)
    whole_angle = (
        2.0
        * math.pi
        / total_len
        * (coarse_freq[:, None] * fine_index[None, :] % total_len).astype(jnp.float32)
    )
    whole_cos = jnp.cos(whole_angle)[:, :, None]
    whole_sin = jnp.sin(whole_angle)[:, :, None]
    first_real = product_einsum("kn,nrc->krc", coarse_cos, blocks)
    first_imag = -product_einsum("kn,nrc->krc", coarse_sin, blocks)
    turned_real = first_real * whole_cos + first_imag * whole_sin
    turned_imag = first_imag * whole_cos - first_real * whole_sin
    spec_real = product_einsum("kn,jnc->kjc", fine_cos, turned_real) + product_einsum(
        "kn,jnc->kjc", fine_sin, turned_imag
    )
    spec_imag = product_einsum("kn,jnc->kjc", fine_cos, turned_imag) - product_einsum(
        "kn,jnc->kjc", fine_sin, turned_real
    )
    resp_grid = resp_narrow.reshape(2, seq_rows, coarse_len, narrow_width)
    kept_real = spec_real * resp_grid[0] - spec_imag * resp_grid[1]
    kept_imag = spec_real * resp_grid[1] + spec_imag * resp_grid[0]
    back_real = product_einsum("kn,kjc->jnc", fine_cos, kept_real) - product_einsum(
        "kn,kjc->jnc", fine_sin, kept_imag
    )
    back_imag = product_einsum("kn,kjc->jnc", fine_cos, kept_imag) + product_einsum(
        "kn,kjc->jnc", fine_sin, kept_real
    )
    untwist_real = back_real * whole_cos - back_imag * whole_sin
    untwist_imag = back_real * whole_sin + back_imag * whole_cos
    inverse_part = (
        product_einsum("kn,krc->nrc", coarse_cos, untwist_real)
        - product_einsum("kn,krc->nrc", coarse_sin, untwist_imag)
    ) * (1.0 / total_len)
    filtered = lax.all_to_all(
        inverse_part.reshape(seq_parts * seq_rows, narrow_width).astype(jnp.bfloat16),
        "seq",
        split_axis=0,
        concat_axis=1,
        tiled=True,
    ).astype(jnp.float32)
    gated = (query * (filtered + skip_gain[None, :] * signal)).astype(jnp.bfloat16)
    partial_terms = jnp.dot(gated, out_weight, preferred_element_type=jnp.float32)
    return lax.psum_scatter(
        partial_terms.astype(jnp.bfloat16), "chan", scatter_dimension=1, tiled=True
    )


def per_device(projected, short_taps, skip_gain, filter_response, out_weight):
    parts = lax.axis_size("seq")
    rows, width = projected.shape[1:]
    fits = (
        parts == 8
        and lax.axis_size("chan") == 4
        and width == parts // 2 * LANES
        and rows % 128 == 0
        and filter_response.shape[1] == 2 * rows
        and out_weight.shape[1] % (16 * LANES) == 0
    )
    form = per_device_kernel if fits else per_device_collectives
    return form(projected, short_taps, skip_gain, filter_response, out_weight)


def solution(mesh):
    placed = (
        P(None, "seq", "chan"),
        P(None, None, "chan"),
        P("chan"),
        P(None, "seq", "chan"),
        P("chan", None),
    )
    return jax.shard_map(
        per_device, mesh=mesh, in_specs=placed, out_specs=P("seq", "chan"), check_vma=False
    )
```

```python
import functools
import math

import jax
import jax.numpy as jnp
import numpy as np
from jax import lax
from jax.experimental import pallas as pl
from jax.experimental.pallas import tpu as pltpu
from jax.sharding import PartitionSpec as P

LANES = 128
MESH = pl.DeviceIdType.MESH


def dft_tables(rows, parts):
    coarse = 2 * parts
    total = coarse * rows
    half = rows // 2
    r = np.arange(rows)[None, :]
    k = np.arange(half)[:, None]

    def pair(j):
        angle = 2.0 * np.pi * ((r * (coarse * k + j)) % total) / total
        return np.cos(angle), np.sin(angle)

    tables = np.zeros((parts, 2 * rows, 2 * rows), np.float32)
    cos0, sin0 = pair(0)
    cosn, sinn = pair(parts)
    tables[0, :half, :rows] = cos0
    tables[0, half:rows, :rows] = -sin0
    tables[0, rows : rows + half, rows:] = cosn
    tables[0, rows + half :, rows:] = -sinn
    for m in range(1, parts):
        c, s = pair(m)
        tables[m, :rows] = np.block([[c, s], [-s, c]])
        c, s = pair(coarse - m)
        tables[m, rows:] = np.block([[c, -s], [-s, -c]])
    return tables.astype(jnp.bfloat16)


def regroup_matrix(count, coarse):
    fine = count // coarse
    matrix = np.zeros((count, count), np.float32)
    out = np.arange(count)
    matrix[out, (out % fine) * coarse + out // fine] = 1.0
    return matrix.astype(jnp.bfloat16)


def weighted(terms):
    total = None
    for weight, value in terms:
        if abs(weight) < 1e-12:
            continue
        if abs(weight - 1.0) < 1e-12:
            part = value
        elif abs(weight + 1.0) < 1e-12:
            part = -value
        else:
            part = value * weight
        total = part if total is None else total + part
    return total


def layer_kernel(
    parts, pieces, row_chunks,
    proj_hbm, taps_ref, skip_ref, filt_hbm, weight_hbm, tables_hbm, regroup_hbm,
    out_hbm,
    proj, filt, weight, tables, regroup, rim,
    query, signal, signal_bf, heard, filt_bf, resp,
    coarse_in, spectrum, inverse, narrow_out, returned, gated,
    side_out, side_in, far_out, far_in, side_own_out, side_own_in, own_sum, mixed,
    load_sem, rim_sem, sig_send, sig_recv, filt_send, filt_recv,
    back_send, back_recv, side_sems, far_sems, own_sems, store_sems,
):
    seq = lax.axis_index("seq")
    chan = lax.axis_index("chan")
    groups = parts // 2
    half = seq // groups
    group = seq % groups
    sibling = chan + 1 - 2 * (chan % 2)
    across = (chan + 2) % 4
    diagonal = (sibling + 2) % 4
    rows = proj.shape[1]
    coarse = 2 * parts
    half_rows = rows // 2
    fine_held = filt.shape[1] // coarse
    out_width = mixed.shape[1]
    piece = out_width // pieces

    barrier = pltpu.get_barrier_semaphore()
    for o in range(1, parts):
        pl.semaphore_signal(barrier, inc=1, device_id={"seq": (seq + o) % parts}, device_id_type=MESH)
    for partner in (sibling, across):
        pl.semaphore_signal(barrier, inc=1, device_id={"chan": partner}, device_id_type=MESH)

    load_proj = pltpu.make_async_copy(proj_hbm, proj, load_sem.at[0])
    load_proj.start()
    load_regroup = pltpu.make_async_copy(regroup_hbm, regroup, load_sem.at[5])
    load_regroup.start()
    load_filt = []
    for p in range(2):
        load_filt.append(pltpu.make_async_copy(filt_hbm.at[p], filt.at[p], load_sem.at[1 + p]))
        load_filt[-1].start()
    load_tables = pltpu.make_async_copy(tables_hbm, tables, load_sem.at[3])
    load_weight = pltpu.make_async_copy(weight_hbm, weight, load_sem.at[4])

    load_proj.wait()
    pl.semaphore_wait(barrier, parts + 1)
    rim_copy = pltpu.make_async_remote_copy(
        src_ref=proj.at[:, pl.ds(rows - 16, 16), :],
        dst_ref=rim,
        send_sem=rim_sem.at[0],
        recv_sem=rim_sem.at[1],
        device_id={"seq": (seq + 1) % parts},
        device_id_type=MESH,
    )
    rim_copy.start()

    filt_copies = []

    def send_filter(p):
        load_filt[p].wait()
        filt_bf[p] = jnp.dot(
            regroup[...], filt[p].astype(jnp.bfloat16), preferred_element_type=jnp.float32
        ).astype(jnp.bfloat16)
        for o in range(1, groups):
            target = (group + o) % groups
            columns = pl.ds(pl.multiple_of(target * LANES, LANES), LANES)
            copy = pltpu.make_async_remote_copy(
                src_ref=filt_bf.at[p, :, columns],
                dst_ref=resp.at[group, p],
                send_sem=filt_send.at[p, o],
                recv_sem=filt_recv.at[p, o],
                device_id={"seq": half * groups + target},
                device_id_type=MESH,
            )
            copy.start()
            filt_copies.append(copy)

    def shaped(i, columns, count, fixed):
        now = proj[i, :count, columns].astype(jnp.float32)
        one, two = pltpu.roll(now, 1, 0), pltpu.roll(now, 2, 0)
        if fixed:
            row_index = lax.broadcasted_iota(jnp.int32, now.shape, 0)
            edge = rim[i, :, columns].astype(jnp.float32)
            edge = jnp.where(seq == 0, jnp.zeros_like(edge), edge)
            last, before = edge[15:16], edge[14:15]
            one = jnp.where(row_index == 0, last, one)
            two = jnp.where(row_index == 0, before, jnp.where(row_index == 1, last, two))
        return (
            taps_ref[i, 0:1, columns] * now
            + taps_ref[i, 1:2, columns] * one
            + taps_ref[i, 2:3, columns] * two
        )

    def shape_signal(count, fixed):
        for g in range(groups):
            columns = slice(g * LANES, (g + 1) * LANES)
            value = shaped(1, columns, count, fixed) * shaped(2, columns, count, fixed)
            signal[:count, columns] = value
            signal_bf[:count, columns] = value.astype(jnp.bfloat16)

    def shape_query(count, fixed):
        for g in range(groups):
            columns = slice(g * LANES, (g + 1) * LANES)
            query[:count, columns] = shaped(0, columns, count, fixed)

    shape_signal(rows, False)
    load_regroup.wait()
    send_filter(0)
    rim_copy.wait()
    shape_signal(16, True)

    own_columns = pl.ds(pl.multiple_of(group * LANES, LANES), LANES)
    sig_copies = []
    for o in sorted(range(1, parts), key=lambda o: abs(o - groups)):
        target = (seq + o) % parts
        columns = pl.ds(pl.multiple_of((target % groups) * LANES, LANES), LANES)
        copy = pltpu.make_async_remote_copy(
            src_ref=signal_bf.at[:, columns],
            dst_ref=heard.at[seq],
            send_sem=sig_send.at[o],
            recv_sem=sig_recv.at[o],
            device_id={"seq": target},
            device_id_type=MESH,
        )
        copy.start()
        sig_copies.append(copy)
    heard[seq] = signal_bf[:, own_columns]
    send_filter(1)
    load_tables.start()
    load_weight.start()
    for p in range(2):
        resp[group, p] = filt_bf[p, :, own_columns]
    shape_query(rows, False)
    shape_query(16, True)

    for copy in sig_copies:
        copy.wait_recv()

    chunk = 32

    def parity(start):
        index = lax.broadcasted_iota(jnp.int32, (chunk, LANES), 0)
        return (1 - 2 * half * (index % 2)).astype(jnp.float32)

    angle = 2.0 * math.pi / coarse

    def forward(step, carry):
        start = pl.multiple_of(step * chunk, chunk)
        sign = parity(start)
        x = [heard[n, pl.ds(start, chunk), :].astype(jnp.float32) * sign for n in range(parts)]
        for m in range(parts):
            if m == 0:
                real = weighted([(1.0, x[n]) for n in range(parts)])
                imag = weighted([((-1.0) ** n, x[n]) for n in range(parts)])
            else:
                real = weighted([(math.cos(angle * m * n), x[n]) for n in range(parts)])
                imag = weighted([(-math.sin(angle * m * n), x[n]) for n in range(parts)])
            coarse_in[m, pl.ds(start, chunk), :] = real.astype(jnp.bfloat16)
            coarse_in[m, pl.ds(rows + start, chunk), :] = imag.astype(jnp.bfloat16)
        return carry

    lax.fori_loop(0, rows // chunk, forward, 0)
    load_tables.wait()
    for m in range(parts):
        spectrum[m] = jnp.dot(tables[m], coarse_in[m], preferred_element_type=jnp.float32)

    for copy in filt_copies:
        copy.wait_recv()

    for m in range(parts):
        kept = []
        for at, j in ((0, m), (rows, parts if m == 0 else coarse - m)):
            real = spectrum[m, at : at + half_rows]
            imag = spectrum[m, at + half_rows : at + rows]
            held = slice(j * fine_held, (j + 1) * fine_held)
            resp_real = jnp.concatenate([resp[g, 0, held] for g in range(groups)], 0).astype(jnp.float32)
            resp_imag = jnp.concatenate([resp[g, 1, held] for g in range(groups)], 0).astype(jnp.float32)
            kept.append((real * resp_real - imag * resp_imag).astype(jnp.bfloat16))
            kept.append((real * resp_imag + imag * resp_real).astype(jnp.bfloat16))
        inverse[m] = lax.dot_general(
            tables[m], jnp.concatenate(kept, 0), (((0,), (0,)), ((), ())), preferred_element_type=jnp.float32
        )

    def backward(step, carry):
        start = pl.multiple_of(step * chunk, chunk)
        sign = parity(start) * (1.0 / (coarse * rows))
        real = [inverse[m, pl.ds(start, chunk), :] for m in range(parts)]
        imag = [inverse[m, pl.ds(rows + start, chunk), :] for m in range(parts)]
        for n in range(parts):
            terms = [(1.0, real[0]), ((-1.0) ** n, imag[0])]
            for m in range(1, parts):
                terms.append((math.cos(angle * m * n), real[m]))
                terms.append((-math.sin(angle * m * n), imag[m]))
            narrow_out[n, pl.ds(start, chunk), :] = (weighted(terms) * sign).astype(jnp.bfloat16)
        return carry

    back_copies = []

    def start_back(t):
        first, count = row_chunks[t]
        here = pl.ds(first, count)
        back_copies.append([])
        for o in sorted(range(1, parts), key=lambda o: abs(o - groups)):
            target = (seq + o) % parts
            copy = pltpu.make_async_remote_copy(
                src_ref=narrow_out.at[target, here],
                dst_ref=returned.at[seq, here],
                send_sem=back_send.at[t, o],
                recv_sem=back_recv.at[t, o],
                device_id={"seq": target},
                device_id_type=MESH,
            )
            copy.start()
            back_copies[t].append(copy)

    def next_back():
        t = len(back_copies)
        if t < len(row_chunks):
            for copy in back_copies[t - 1]:
                copy.wait_send()
            start_back(t)

    lax.fori_loop(0, row_chunks[0][1] // chunk, backward, 0)
    start_back(0)
    lax.fori_loop(row_chunks[0][1] // chunk, rows // chunk, backward, 0)
    next_back()
    returned[seq] = narrow_out[seq]
    load_weight.wait()

    def send(source, target_ref, sems, at, part, partner):
        rows_at, columns = part
        copy = pltpu.make_async_remote_copy(
            src_ref=source.at[rows_at, columns],
            dst_ref=target_ref.at[rows_at, columns],
            send_sem=sems.at[0, at],
            recv_sem=sems.at[1, at],
            device_id={"chan": partner},
            device_id_type=MESH,
        )
        copy.start()
        return copy

    side_copies, far_copies, own_copies, all_parts = [], [], [], []
    for t, (first, count) in enumerate(row_chunks):
        for copy in back_copies[t]:
            copy.wait_recv()
        here = slice(first, first + count)
        for g in range(groups):
            columns = slice(g * LANES, (g + 1) * LANES)
            filtered = returned[g, here].astype(jnp.float32) + returned[groups + g, here].astype(jnp.float32)
            gated[here, columns] = (
                query[here, columns] * (filtered + skip_ref[:, columns] * signal[here, columns])
            ).astype(jnp.bfloat16)

        def product(block, c):
            columns = pl.ds(pl.multiple_of(block * out_width + c * piece, piece), piece)
            return jnp.dot(gated[here], weight[:, columns], preferred_element_type=jnp.float32)

        base = len(all_parts)
        parts_here = [(pl.ds(first, count), pl.ds(c * piece, piece)) for c in range(pieces)]
        all_parts += parts_here
        for c, part in enumerate(parts_here):
            side_out[part] = product(diagonal, c).astype(jnp.bfloat16)
            side_copies.append(send(side_out, side_in, side_sems, base + c, part, sibling))
        for c, part in enumerate(parts_here):
            mine = product(across, c)
            side_copies[base + c].wait_recv()
            far_out[part] = (mine + side_in[part].astype(jnp.float32)).astype(jnp.bfloat16)
            far_copies.append(send(far_out, far_in, far_sems, base + c, part, across))
        next_back()
        for c, part in enumerate(parts_here):
            side_own_out[part] = product(sibling, c).astype(jnp.bfloat16)
            own_copies.append(send(side_own_out, side_own_in, own_sems, base + c, part, sibling))
        for c, part in enumerate(parts_here):
            own_sum[part] = product(chan, c)
    stores = []
    for at, part in enumerate(all_parts):
        own_copies[at].wait_recv()
        far_copies[at].wait_recv()
        mixed[part] = (
            own_sum[part] + side_own_in[part].astype(jnp.float32) + far_in[part].astype(jnp.float32)
        ).astype(jnp.bfloat16)
        stores.append(pltpu.make_async_copy(mixed.at[part], out_hbm.at[part], store_sems.at[at]))
        stores[-1].start()
    for copy in filt_copies + sig_copies + back_copies[-1] + side_copies + far_copies + own_copies:
        copy.wait_send()
    for copy in stores:
        copy.wait()


def place_kernel(source, target, held, loads, stores):
    slabs = loads.shape[0]
    rows = source.shape[0] // slabs
    steps = []
    for i in range(slabs):
        here = pl.ds(i * rows, rows)
        steps.append(
            (
                pltpu.make_async_copy(source.at[here], held.at[here], loads.at[i]),
                pltpu.make_async_copy(held.at[here], target.at[here], stores.at[i]),
            )
        )
        steps[-1][0].start()
    for load, store in steps:
        load.wait()
        store.start()
    for load, store in steps:
        store.wait()


def per_device_kernel(projected, short_taps, skip_gain, filter_response, out_weight):
    parts = lax.axis_size("seq")
    chans = lax.axis_size("chan")
    rows, width = projected.shape[1:]
    held = filter_response.shape[1]
    out_width = out_weight.shape[1] // chans
    groups = parts // 2
    pieces = 2
    quarter = rows // 4
    row_chunks = ((0, quarter), (quarter, quarter), (2 * quarter, 2 * quarter))
    count = pieces * len(row_chunks)
    bf, f32 = jnp.bfloat16, jnp.float32
    any_spec = pl.BlockSpec(memory_space=pl.ANY)
    vmem_spec = pl.BlockSpec(memory_space=pltpu.VMEM)
    dma = pltpu.SemaphoreType.DMA
    exchange = pltpu.VMEM((rows, out_width), bf)
    mixed = pl.pallas_call(
        functools.partial(layer_kernel, parts, pieces, row_chunks),
        out_shape=jax.ShapeDtypeStruct((rows, out_width), bf),
        in_specs=[any_spec, vmem_spec, vmem_spec, any_spec, any_spec, any_spec, any_spec],
        out_specs=any_spec,
        scratch_shapes=[
            pltpu.VMEM((3, rows, width), bf),
            pltpu.VMEM((2, held, width), f32),
            pltpu.VMEM(out_weight.shape, bf),
            pltpu.VMEM((parts, 2 * rows, 2 * rows), bf),
            pltpu.VMEM((held, held), bf),
            pltpu.VMEM((3, 16, width), bf),
            pltpu.VMEM((rows, width), f32),
            pltpu.VMEM((rows, width), f32),
            pltpu.VMEM((rows, width), bf),
            pltpu.VMEM((parts, rows, LANES), bf),
            pltpu.VMEM((2, held, width), bf),
            pltpu.VMEM((groups, 2, held, LANES), bf),
            pltpu.VMEM((parts, 2 * rows, LANES), bf),
            pltpu.VMEM((parts, 2 * rows, LANES), f32),
            pltpu.VMEM((parts, 2 * rows, LANES), f32),
            pltpu.VMEM((parts, rows, LANES), bf),
            pltpu.VMEM((parts, rows, LANES), bf),
            pltpu.VMEM((rows, width), bf),
            exchange, exchange, exchange, exchange, exchange, exchange,
            pltpu.VMEM((rows, out_width), f32),
            pltpu.VMEM((rows, out_width), bf),
            dma((6,)), dma((2,)),
            dma((parts,)), dma((parts,)),
            dma((2, groups)), dma((2, groups)),
            dma((len(row_chunks), parts)), dma((len(row_chunks), parts)),
            dma((2, count)), dma((2, count)), dma((2, count)), dma((count,)),
        ],
        compiler_params=pltpu.CompilerParams(
            collective_id=0, has_side_effects=True, vmem_limit_bytes=56 * 1024 * 1024
        ),
    )(
        projected,
        short_taps,
        skip_gain.reshape(1, width),
        filter_response,
        out_weight,
        jnp.asarray(dft_tables(rows, parts)),
        jnp.asarray(regroup_matrix(held, 2 * parts)),
    )
    return pl.pallas_call(
        place_kernel,
        out_shape=jax.ShapeDtypeStruct(mixed.shape, mixed.dtype),
        in_specs=[any_spec],
        out_specs=any_spec,
        scratch_shapes=[pltpu.VMEM(mixed.shape, mixed.dtype), dma((4,)), dma((4,))],
    )(mixed)


def shifted(value, axis, steps):
    count = lax.axis_size(axis)
    first, last = (max(0, -steps), min(count, count - steps))
    return lax.ppermute(value, axis, [(source, source + steps) for source in range(first, last)])


def product_einsum(form, left, right):
    return jnp.einsum(form, left, right, precision=lax.Precision.HIGHEST)


def per_device_collectives(projected, short_taps, skip_gain, filter_response, out_weight):
    seq_rows = projected.shape[1]
    seq_parts = lax.axis_size("seq")
    coarse_len = 2 * seq_parts
    total_len = coarse_len * seq_rows
    rim_rows = shifted(projected[:, seq_rows - 2 :, :], "seq", 1)
    padded = jnp.concatenate([rim_rows, projected], axis=1).astype(jnp.float32)
    shaped = (
        short_taps[:, 0, None, :] * padded[:, 2:]
        + short_taps[:, 1, None, :] * padded[:, 1:-1]
        + short_taps[:, 2, None, :] * padded[:, :-2]
    )
    query = shaped[0]
    signal = shaped[1] * shaped[2]
    coarse_freq = jnp.arange(coarse_len, dtype=jnp.int32)
    coarse_pos = jnp.arange(seq_parts, dtype=jnp.int32)
    coarse_angle = (
        2.0
        * math.pi
        / coarse_len
        * (coarse_freq[:, None] * coarse_pos[None, :] % coarse_len).astype(jnp.float32)
    )
    coarse_cos = jnp.cos(coarse_angle)
    coarse_sin = jnp.sin(coarse_angle)
    fine_index = jnp.arange(seq_rows, dtype=jnp.int32)
    fine_angle = (
        2.0
        * math.pi
        / seq_rows
        * (fine_index[:, None] * fine_index[None, :] % seq_rows).astype(jnp.float32)
    )
    fine_cos = jnp.cos(fine_angle)
    fine_sin = jnp.sin(fine_angle)
    narrow = lax.all_to_all(
        signal.astype(jnp.bfloat16), "seq", split_axis=1, concat_axis=0, tiled=True
    ).astype(signal.dtype)
    resp_narrow = lax.all_to_all(
        filter_response.astype(jnp.bfloat16), "seq", split_axis=2, concat_axis=1, tiled=True
    ).astype(filter_response.dtype)
    narrow_width = narrow.shape[1]
    blocks = narrow.reshape(seq_parts, seq_rows, narrow_width)
    whole_angle = (
        2.0
        * math.pi
        / total_len
        * (coarse_freq[:, None] * fine_index[None, :] % total_len).astype(jnp.float32)
    )
    whole_cos = jnp.cos(whole_angle)[:, :, None]
    whole_sin = jnp.sin(whole_angle)[:, :, None]
    first_real = product_einsum("kn,nrc->krc", coarse_cos, blocks)
    first_imag = -product_einsum("kn,nrc->krc", coarse_sin, blocks)
    turned_real = first_real * whole_cos + first_imag * whole_sin
    turned_imag = first_imag * whole_cos - first_real * whole_sin
    spec_real = product_einsum("kn,jnc->kjc", fine_cos, turned_real) + product_einsum(
        "kn,jnc->kjc", fine_sin, turned_imag
    )
    spec_imag = product_einsum("kn,jnc->kjc", fine_cos, turned_imag) - product_einsum(
        "kn,jnc->kjc", fine_sin, turned_real
    )
    resp_grid = resp_narrow.reshape(2, seq_rows, coarse_len, narrow_width)
    kept_real = spec_real * resp_grid[0] - spec_imag * resp_grid[1]
    kept_imag = spec_real * resp_grid[1] + spec_imag * resp_grid[0]
    back_real = product_einsum("kn,kjc->jnc", fine_cos, kept_real) - product_einsum(
        "kn,kjc->jnc", fine_sin, kept_imag
    )
    back_imag = product_einsum("kn,kjc->jnc", fine_cos, kept_imag) + product_einsum(
        "kn,kjc->jnc", fine_sin, kept_real
    )
    untwist_real = back_real * whole_cos - back_imag * whole_sin
    untwist_imag = back_real * whole_sin + back_imag * whole_cos
    inverse_part = (
        product_einsum("kn,krc->nrc", coarse_cos, untwist_real)
        - product_einsum("kn,krc->nrc", coarse_sin, untwist_imag)
    ) * (1.0 / total_len)
    filtered = lax.all_to_all(
        inverse_part.reshape(seq_parts * seq_rows, narrow_width).astype(jnp.bfloat16),
        "seq",
        split_axis=0,
        concat_axis=1,
        tiled=True,
    ).astype(jnp.float32)
    gated = (query * (filtered + skip_gain[None, :] * signal)).astype(jnp.bfloat16)
    partial_terms = jnp.dot(gated, out_weight, preferred_element_type=jnp.float32)
    return lax.psum_scatter(
        partial_terms.astype(jnp.bfloat16), "chan", scatter_dimension=1, tiled=True
    )


def per_device(projected, short_taps, skip_gain, filter_response, out_weight):
    parts = lax.axis_size("seq")
    rows, width = projected.shape[1:]
    fits = (
        parts == 8
        and lax.axis_size("chan") == 4
        and width == parts // 2 * LANES
        and rows % 128 == 0
        and filter_response.shape[1] == 2 * rows
        and out_weight.shape[1] % (16 * LANES) == 0
    )
    form = per_device_kernel if fits else per_device_collectives
    return form(projected, short_taps, skip_gain, filter_response, out_weight)


def solution(mesh):
    placed = (
        P(None, "seq", "chan"),
        P(None, None, "chan"),
        P("chan"),
        P(None, "seq", "chan"),
        P("chan", None),
    )
    return jax.shard_map(
        per_device, mesh=mesh, in_specs=placed, out_specs=P("seq", "chan"), check_vma=False
    )
```

```python
import functools
import math

import jax
import jax.numpy as jnp
import numpy as np
from jax import lax
from jax.experimental import pallas as pl
from jax.experimental.pallas import tpu as pltpu
from jax.sharding import PartitionSpec as P

LANES = 128
MESH = pl.DeviceIdType.MESH


def dft_tables(rows, parts):
    coarse = 2 * parts
    total = coarse * rows
    half = rows // 2
    r = np.arange(rows)[None, :]
    k = np.arange(half)[:, None]

    def pair(j):
        angle = 2.0 * np.pi * ((r * (coarse * k + j)) % total) / total
        return np.cos(angle), np.sin(angle)

    tables = np.zeros((parts, 2 * rows, 2 * rows), np.float32)
    cos0, sin0 = pair(0)
    cosn, sinn = pair(parts)
    tables[0, :half, :rows] = cos0
    tables[0, half:rows, :rows] = -sin0
    tables[0, rows : rows + half, rows:] = cosn
    tables[0, rows + half :, rows:] = -sinn
    for m in range(1, parts):
        c, s = pair(m)
        tables[m, :rows] = np.block([[c, s], [-s, c]])
        c, s = pair(coarse - m)
        tables[m, rows:] = np.block([[c, -s], [-s, -c]])
    return tables.astype(jnp.bfloat16)


def regroup_matrix(count, coarse):
    fine = count // coarse
    matrix = np.zeros((count, count), np.float32)
    out = np.arange(count)
    matrix[out, (out % fine) * coarse + out // fine] = 1.0
    return matrix.astype(jnp.bfloat16)


def weighted(terms):
    total = None
    for weight, value in terms:
        if abs(weight) < 1e-12:
            continue
        if abs(weight - 1.0) < 1e-12:
            part = value
        elif abs(weight + 1.0) < 1e-12:
            part = -value
        else:
            part = value * weight
        total = part if total is None else total + part
    return total


def layer_kernel(
    parts, pieces, row_chunks,
    proj_hbm, taps_ref, skip_ref, filt_hbm, weight_hbm, tables_hbm, turned_hbm, regroup_hbm,
    out_hbm,
    proj, filt, weight, tables, turned, regroup, rim,
    query, signal, signal_bf, heard, filt_bf, resp,
    coarse_in, spectrum, inverse, narrow_out, returned, gated,
    side_out, side_in, far_out, far_in, side_own_out, side_own_in, own_sum, mixed,
    load_sem, rim_sem, sig_send, sig_recv, filt_send, filt_recv,
    back_send, back_recv, side_sems, far_sems, own_sems, store_sems,
):
    seq = lax.axis_index("seq")
    chan = lax.axis_index("chan")
    groups = parts // 2
    half = seq // groups
    group = seq % groups
    sibling = chan + 1 - 2 * (chan % 2)
    across = (chan + 2) % 4
    diagonal = (sibling + 2) % 4
    rows = proj.shape[1]
    coarse = 2 * parts
    half_rows = rows // 2
    fine_held = filt.shape[1] // coarse
    out_width = mixed.shape[1]
    piece = out_width // pieces

    barrier = pltpu.get_barrier_semaphore()
    for o in range(1, parts):
        pl.semaphore_signal(barrier, inc=1, device_id={"seq": (seq + o) % parts}, device_id_type=MESH)
    for partner in (sibling, across):
        pl.semaphore_signal(barrier, inc=1, device_id={"chan": partner}, device_id_type=MESH)

    load_proj = pltpu.make_async_copy(proj_hbm, proj, load_sem.at[0])
    load_proj.start()
    load_regroup = pltpu.make_async_copy(regroup_hbm, regroup, load_sem.at[5])
    load_regroup.start()
    load_filt = []
    for p in range(2):
        load_filt.append(pltpu.make_async_copy(filt_hbm.at[p], filt.at[p], load_sem.at[1 + p]))
        load_filt[-1].start()
    load_tables = pltpu.make_async_copy(tables_hbm, tables, load_sem.at[3])
    load_weight = pltpu.make_async_copy(weight_hbm, weight, load_sem.at[4])

    load_proj.wait()
    pl.semaphore_wait(barrier, parts + 1)
    rim_copy = pltpu.make_async_remote_copy(
        src_ref=proj.at[:, pl.ds(rows - 16, 16), :],
        dst_ref=rim,
        send_sem=rim_sem.at[0],
        recv_sem=rim_sem.at[1],
        device_id={"seq": (seq + 1) % parts},
        device_id_type=MESH,
    )
    rim_copy.start()

    filt_copies = []

    def send_filter(p):
        load_filt[p].wait()
        filt_bf[p] = jnp.dot(
            regroup[...], filt[p].astype(jnp.bfloat16), preferred_element_type=jnp.float32
        ).astype(jnp.bfloat16)
        for o in range(1, groups):
            target = (group + o) % groups
            columns = pl.ds(pl.multiple_of(target * LANES, LANES), LANES)
            copy = pltpu.make_async_remote_copy(
                src_ref=filt_bf.at[p, :, columns],
                dst_ref=resp.at[group, p],
                send_sem=filt_send.at[p, o],
                recv_sem=filt_recv.at[p, o],
                device_id={"seq": half * groups + target},
                device_id_type=MESH,
            )
            copy.start()
            filt_copies.append(copy)

    def shaped(i, columns, count, fixed):
        now = proj[i, :count, columns].astype(jnp.float32)
        one, two = pltpu.roll(now, 1, 0), pltpu.roll(now, 2, 0)
        if fixed:
            row_index = lax.broadcasted_iota(jnp.int32, now.shape, 0)
            edge = rim[i, :, columns].astype(jnp.float32)
            edge = jnp.where(seq == 0, jnp.zeros_like(edge), edge)
            last, before = edge[15:16], edge[14:15]
            one = jnp.where(row_index == 0, last, one)
            two = jnp.where(row_index == 0, before, jnp.where(row_index == 1, last, two))
        return (
            taps_ref[i, 0:1, columns] * now
            + taps_ref[i, 1:2, columns] * one
            + taps_ref[i, 2:3, columns] * two
        )

    def shape_signal(count, fixed):
        for g in range(groups):
            columns = slice(g * LANES, (g + 1) * LANES)
            value = shaped(1, columns, count, fixed) * shaped(2, columns, count, fixed)
            signal[:count, columns] = value
            signal_bf[:count, columns] = value.astype(jnp.bfloat16)

    def shape_query(count, fixed):
        for g in range(groups):
            columns = slice(g * LANES, (g + 1) * LANES)
            query[:count, columns] = shaped(0, columns, count, fixed)

    shape_signal(rows, False)
    load_regroup.wait()
    send_filter(0)
    rim_copy.wait()
    shape_signal(16, True)

    own_columns = pl.ds(pl.multiple_of(group * LANES, LANES), LANES)
    sig_copies = []
    for o in sorted(range(1, parts), key=lambda o: abs(o - groups)):
        target = (seq + o) % parts
        columns = pl.ds(pl.multiple_of((target % groups) * LANES, LANES), LANES)
        copy = pltpu.make_async_remote_copy(
            src_ref=signal_bf.at[:, columns],
            dst_ref=heard.at[seq],
            send_sem=sig_send.at[o],
            recv_sem=sig_recv.at[o],
            device_id={"seq": target},
            device_id_type=MESH,
        )
        copy.start()
        sig_copies.append(copy)
    heard[seq] = signal_bf[:, own_columns]
    send_filter(1)
    load_tables.start()
    load_turned = pltpu.make_async_copy(turned_hbm, turned, load_sem.at[6])
    load_turned.start()
    load_weight.start()
    for p in range(2):
        resp[group, p] = filt_bf[p, :, own_columns]
    shape_query(rows, False)
    shape_query(16, True)

    for copy in sig_copies:
        copy.wait_recv()

    chunk = 32

    def parity(start):
        index = lax.broadcasted_iota(jnp.int32, (chunk, LANES), 0)
        return (1 - 2 * half * (index % 2)).astype(jnp.float32)

    angle = 2.0 * math.pi / coarse

    def forward(step, carry):
        start = pl.multiple_of(step * chunk, chunk)
        sign = parity(start)
        x = [heard[n, pl.ds(start, chunk), :].astype(jnp.float32) * sign for n in range(parts)]
        for m in range(parts):
            if m == 0:
                real = weighted([(1.0, x[n]) for n in range(parts)])
                imag = weighted([((-1.0) ** n, x[n]) for n in range(parts)])
            else:
                real = weighted([(math.cos(angle * m * n), x[n]) for n in range(parts)])
                imag = weighted([(-math.sin(angle * m * n), x[n]) for n in range(parts)])
            coarse_in[m, pl.ds(start, chunk), :] = real.astype(jnp.bfloat16)
            coarse_in[m, pl.ds(rows + start, chunk), :] = imag.astype(jnp.bfloat16)
        return carry

    lax.fori_loop(0, rows // chunk, forward, 0)
    load_tables.wait()
    for m in range(parts):
        spectrum[m] = jnp.dot(tables[m], coarse_in[m], preferred_element_type=jnp.float32)

    load_turned.wait()
    for copy in filt_copies:
        copy.wait_recv()

    for m in range(parts):
        kept = []
        for at, j in ((0, m), (rows, parts if m == 0 else coarse - m)):
            real = spectrum[m, at : at + half_rows]
            imag = spectrum[m, at + half_rows : at + rows]
            held = slice(j * fine_held, (j + 1) * fine_held)
            resp_real = jnp.concatenate([resp[g, 0, held] for g in range(groups)], 0).astype(jnp.float32)
            resp_imag = jnp.concatenate([resp[g, 1, held] for g in range(groups)], 0).astype(jnp.float32)
            kept.append((real * resp_real - imag * resp_imag).astype(jnp.bfloat16))
            kept.append((real * resp_imag + imag * resp_real).astype(jnp.bfloat16))
        inverse[m] = jnp.dot(turned[m], jnp.concatenate(kept, 0), preferred_element_type=jnp.float32)

    def backward(step, carry):
        start = pl.multiple_of(step * chunk, chunk)
        sign = parity(start) * (1.0 / (coarse * rows))
        real = [inverse[m, pl.ds(start, chunk), :] for m in range(parts)]
        imag = [inverse[m, pl.ds(rows + start, chunk), :] for m in range(parts)]
        for n in range(parts):
            terms = [(1.0, real[0]), ((-1.0) ** n, imag[0])]
            for m in range(1, parts):
                terms.append((math.cos(angle * m * n), real[m]))
                terms.append((-math.sin(angle * m * n), imag[m]))
            narrow_out[n, pl.ds(start, chunk), :] = (weighted(terms) * sign).astype(jnp.bfloat16)
        return carry

    back_copies = []

    def start_back(t):
        first, count = row_chunks[t]
        here = pl.ds(first, count)
        back_copies.append([])
        for o in sorted(range(1, parts), key=lambda o: abs(o - groups)):
            target = (seq + o) % parts
            copy = pltpu.make_async_remote_copy(
                src_ref=narrow_out.at[target, here],
                dst_ref=returned.at[seq, here],
                send_sem=back_send.at[t, o],
                recv_sem=back_recv.at[t, o],
                device_id={"seq": target},
                device_id_type=MESH,
            )
            copy.start()
            back_copies[t].append(copy)

    def next_back():
        t = len(back_copies)
        if t < len(row_chunks):
            for copy in back_copies[t - 1]:
                copy.wait_send()
            start_back(t)

    lax.fori_loop(0, row_chunks[0][1] // chunk, backward, 0)
    start_back(0)
    lax.fori_loop(row_chunks[0][1] // chunk, rows // chunk, backward, 0)
    next_back()
    returned[seq] = narrow_out[seq]
    load_weight.wait()

    def send(source, target_ref, sems, at, part, partner):
        rows_at, columns = part
        copy = pltpu.make_async_remote_copy(
            src_ref=source.at[rows_at, columns],
            dst_ref=target_ref.at[rows_at, columns],
            send_sem=sems.at[0, at],
            recv_sem=sems.at[1, at],
            device_id={"chan": partner},
            device_id_type=MESH,
        )
        copy.start()
        return copy

    side_copies, far_copies, own_copies, all_parts = [], [], [], []
    for t, (first, count) in enumerate(row_chunks):
        for copy in back_copies[t]:
            copy.wait_recv()
        here = slice(first, first + count)
        for g in range(groups):
            columns = slice(g * LANES, (g + 1) * LANES)
            filtered = returned[g, here].astype(jnp.float32) + returned[groups + g, here].astype(jnp.float32)
            gated[here, columns] = (
                query[here, columns] * (filtered + skip_ref[:, columns] * signal[here, columns])
            ).astype(jnp.bfloat16)

        def product(block, c):
            columns = pl.ds(pl.multiple_of(block * out_width + c * piece, piece), piece)
            return jnp.dot(gated[here], weight[:, columns], preferred_element_type=jnp.float32)

        base = len(all_parts)
        parts_here = [(pl.ds(first, count), pl.ds(c * piece, piece)) for c in range(pieces)]
        all_parts += parts_here
        for c, part in enumerate(parts_here):
            side_out[part] = product(diagonal, c).astype(jnp.bfloat16)
            side_copies.append(send(side_out, side_in, side_sems, base + c, part, sibling))
        for c, part in enumerate(parts_here):
            mine = product(across, c)
            side_copies[base + c].wait_recv()
            far_out[part] = (mine + side_in[part].astype(jnp.float32)).astype(jnp.bfloat16)
            far_copies.append(send(far_out, far_in, far_sems, base + c, part, across))
        next_back()
        for c, part in enumerate(parts_here):
            side_own_out[part] = product(sibling, c).astype(jnp.bfloat16)
            own_copies.append(send(side_own_out, side_own_in, own_sems, base + c, part, sibling))
        for c, part in enumerate(parts_here):
            own_sum[part] = product(chan, c)
    stores = []
    for at, part in enumerate(all_parts):
        own_copies[at].wait_recv()
        far_copies[at].wait_recv()
        mixed[part] = (
            own_sum[part] + side_own_in[part].astype(jnp.float32) + far_in[part].astype(jnp.float32)
        ).astype(jnp.bfloat16)
        stores.append(pltpu.make_async_copy(mixed.at[part], out_hbm.at[part], store_sems.at[at]))
        stores[-1].start()
    for copy in filt_copies + sig_copies + back_copies[-1] + side_copies + far_copies + own_copies:
        copy.wait_send()
    for copy in stores:
        copy.wait()


def place_kernel(source, target, held, loads, stores):
    slabs = loads.shape[0]
    rows = source.shape[0] // slabs
    steps = []
    for i in range(slabs):
        here = pl.ds(i * rows, rows)
        steps.append(
            (
                pltpu.make_async_copy(source.at[here], held.at[here], loads.at[i]),
                pltpu.make_async_copy(held.at[here], target.at[here], stores.at[i]),
            )
        )
        steps[-1][0].start()
    for load, store in steps:
        load.wait()
        store.start()
    for load, store in steps:
        store.wait()


def per_device_kernel(projected, short_taps, skip_gain, filter_response, out_weight):
    parts = lax.axis_size("seq")
    chans = lax.axis_size("chan")
    rows, width = projected.shape[1:]
    held = filter_response.shape[1]
    out_width = out_weight.shape[1] // chans
    groups = parts // 2
    pieces = 2
    tables = dft_tables(rows, parts)
    quarter = rows // 4
    row_chunks = ((0, quarter), (quarter, quarter), (2 * quarter, 2 * quarter))
    count = pieces * len(row_chunks)
    bf, f32 = jnp.bfloat16, jnp.float32
    any_spec = pl.BlockSpec(memory_space=pl.ANY)
    vmem_spec = pl.BlockSpec(memory_space=pltpu.VMEM)
    dma = pltpu.SemaphoreType.DMA
    exchange = pltpu.VMEM((rows, out_width), bf)
    mixed = pl.pallas_call(
        functools.partial(layer_kernel, parts, pieces, row_chunks),
        out_shape=jax.ShapeDtypeStruct((rows, out_width), bf),
        in_specs=[any_spec, vmem_spec, vmem_spec, any_spec, any_spec, any_spec, any_spec, any_spec],
        out_specs=any_spec,
        scratch_shapes=[
            pltpu.VMEM((3, rows, width), bf),
            pltpu.VMEM((2, held, width), f32),
            pltpu.VMEM(out_weight.shape, bf),
            pltpu.VMEM((parts, 2 * rows, 2 * rows), bf),
            pltpu.VMEM((parts, 2 * rows, 2 * rows), bf),
            pltpu.VMEM((held, held), bf),
            pltpu.VMEM((3, 16, width), bf),
            pltpu.VMEM((rows, width), f32),
            pltpu.VMEM((rows, width), f32),
            pltpu.VMEM((rows, width), bf),
            pltpu.VMEM((parts, rows, LANES), bf),
            pltpu.VMEM((2, held, width), bf),
            pltpu.VMEM((groups, 2, held, LANES), bf),
            pltpu.VMEM((parts, 2 * rows, LANES), bf),
            pltpu.VMEM((parts, 2 * rows, LANES), f32),
            pltpu.VMEM((parts, 2 * rows, LANES), f32),
            pltpu.VMEM((parts, rows, LANES), bf),
            pltpu.VMEM((parts, rows, LANES), bf),
            pltpu.VMEM((rows, width), bf),
            exchange, exchange, exchange, exchange, exchange, exchange,
            pltpu.VMEM((rows, out_width), f32),
            pltpu.VMEM((rows, out_width), bf),
            dma((7,)), dma((2,)),
            dma((parts,)), dma((parts,)),
            dma((2, groups)), dma((2, groups)),
            dma((len(row_chunks), parts)), dma((len(row_chunks), parts)),
            dma((2, count)), dma((2, count)), dma((2, count)), dma((count,)),
        ],
        compiler_params=pltpu.CompilerParams(
            collective_id=0, has_side_effects=True, vmem_limit_bytes=56 * 1024 * 1024
        ),
    )(
        projected,
        short_taps,
        skip_gain.reshape(1, width),
        filter_response,
        out_weight,
        jnp.asarray(tables),
        jnp.asarray(np.ascontiguousarray(tables.transpose(0, 2, 1))),
        jnp.asarray(regroup_matrix(held, 2 * parts)),
    )
    return pl.pallas_call(
        place_kernel,
        out_shape=jax.ShapeDtypeStruct(mixed.shape, mixed.dtype),
        in_specs=[any_spec],
        out_specs=any_spec,
        scratch_shapes=[pltpu.VMEM(mixed.shape, mixed.dtype), dma((4,)), dma((4,))],
    )(mixed)


def shifted(value, axis, steps):
    count = lax.axis_size(axis)
    first, last = (max(0, -steps), min(count, count - steps))
    return lax.ppermute(value, axis, [(source, source + steps) for source in range(first, last)])


def product_einsum(form, left, right):
    return jnp.einsum(form, left, right, precision=lax.Precision.HIGHEST)


def per_device_collectives(projected, short_taps, skip_gain, filter_response, out_weight):
    seq_rows = projected.shape[1]
    seq_parts = lax.axis_size("seq")
    coarse_len = 2 * seq_parts
    total_len = coarse_len * seq_rows
    rim_rows = shifted(projected[:, seq_rows - 2 :, :], "seq", 1)
    padded = jnp.concatenate([rim_rows, projected], axis=1).astype(jnp.float32)
    shaped = (
        short_taps[:, 0, None, :] * padded[:, 2:]
        + short_taps[:, 1, None, :] * padded[:, 1:-1]
        + short_taps[:, 2, None, :] * padded[:, :-2]
    )
    query = shaped[0]
    signal = shaped[1] * shaped[2]
    coarse_freq = jnp.arange(coarse_len, dtype=jnp.int32)
    coarse_pos = jnp.arange(seq_parts, dtype=jnp.int32)
    coarse_angle = (
        2.0
        * math.pi
        / coarse_len
        * (coarse_freq[:, None] * coarse_pos[None, :] % coarse_len).astype(jnp.float32)
    )
    coarse_cos = jnp.cos(coarse_angle)
    coarse_sin = jnp.sin(coarse_angle)
    fine_index = jnp.arange(seq_rows, dtype=jnp.int32)
    fine_angle = (
        2.0
        * math.pi
        / seq_rows
        * (fine_index[:, None] * fine_index[None, :] % seq_rows).astype(jnp.float32)
    )
    fine_cos = jnp.cos(fine_angle)
    fine_sin = jnp.sin(fine_angle)
    narrow = lax.all_to_all(
        signal.astype(jnp.bfloat16), "seq", split_axis=1, concat_axis=0, tiled=True
    ).astype(signal.dtype)
    resp_narrow = lax.all_to_all(
        filter_response.astype(jnp.bfloat16), "seq", split_axis=2, concat_axis=1, tiled=True
    ).astype(filter_response.dtype)
    narrow_width = narrow.shape[1]
    blocks = narrow.reshape(seq_parts, seq_rows, narrow_width)
    whole_angle = (
        2.0
        * math.pi
        / total_len
        * (coarse_freq[:, None] * fine_index[None, :] % total_len).astype(jnp.float32)
    )
    whole_cos = jnp.cos(whole_angle)[:, :, None]
    whole_sin = jnp.sin(whole_angle)[:, :, None]
    first_real = product_einsum("kn,nrc->krc", coarse_cos, blocks)
    first_imag = -product_einsum("kn,nrc->krc", coarse_sin, blocks)
    turned_real = first_real * whole_cos + first_imag * whole_sin
    turned_imag = first_imag * whole_cos - first_real * whole_sin
    spec_real = product_einsum("kn,jnc->kjc", fine_cos, turned_real) + product_einsum(
        "kn,jnc->kjc", fine_sin, turned_imag
    )
    spec_imag = product_einsum("kn,jnc->kjc", fine_cos, turned_imag) - product_einsum(
        "kn,jnc->kjc", fine_sin, turned_real
    )
    resp_grid = resp_narrow.reshape(2, seq_rows, coarse_len, narrow_width)
    kept_real = spec_real * resp_grid[0] - spec_imag * resp_grid[1]
    kept_imag = spec_real * resp_grid[1] + spec_imag * resp_grid[0]
    back_real = product_einsum("kn,kjc->jnc", fine_cos, kept_real) - product_einsum(
        "kn,kjc->jnc", fine_sin, kept_imag
    )
    back_imag = product_einsum("kn,kjc->jnc", fine_cos, kept_imag) + product_einsum(
        "kn,kjc->jnc", fine_sin, kept_real
    )
    untwist_real = back_real * whole_cos - back_imag * whole_sin
    untwist_imag = back_real * whole_sin + back_imag * whole_cos
    inverse_part = (
        product_einsum("kn,krc->nrc", coarse_cos, untwist_real)
        - product_einsum("kn,krc->nrc", coarse_sin, untwist_imag)
    ) * (1.0 / total_len)
    filtered = lax.all_to_all(
        inverse_part.reshape(seq_parts * seq_rows, narrow_width).astype(jnp.bfloat16),
        "seq",
        split_axis=0,
        concat_axis=1,
        tiled=True,
    ).astype(jnp.float32)
    gated = (query * (filtered + skip_gain[None, :] * signal)).astype(jnp.bfloat16)
    partial_terms = jnp.dot(gated, out_weight, preferred_element_type=jnp.float32)
    return lax.psum_scatter(
        partial_terms.astype(jnp.bfloat16), "chan", scatter_dimension=1, tiled=True
    )


def per_device(projected, short_taps, skip_gain, filter_response, out_weight):
    parts = lax.axis_size("seq")
    rows, width = projected.shape[1:]
    fits = (
        parts == 8
        and lax.axis_size("chan") == 4
        and width == parts // 2 * LANES
        and rows % 128 == 0
        and filter_response.shape[1] == 2 * rows
        and out_weight.shape[1] % (16 * LANES) == 0
    )
    form = per_device_kernel if fits else per_device_collectives
    return form(projected, short_taps, skip_gain, filter_response, out_weight)


def solution(mesh):
    placed = (
        P(None, "seq", "chan"),
        P(None, None, "chan"),
        P("chan"),
        P(None, "seq", "chan"),
        P("chan", None),
    )
    return jax.shard_map(
        per_device, mesh=mesh, in_specs=placed, out_specs=P("seq", "chan"), check_vma=False
    )
```
